32 devices in a mesh: band: 4 (over y, x), patch: 8 (over z, core).
Axes of the slice: x: 2, y: 2, z: 4, core: 2. Of those that a mesh axis runs over, the one named last changes fastest.
Arguments:
- images: float32 [4, 256, 168, 168], P('band', 'patch'), may hold values from -48 to 48
- coeffs: bfloat16 [4, 256, 3, 128, 128], P('band', 'patch'), may hold values from 0.29882812 to 1.5
- inverse_var: float32 [4, 256, 128, 128], P('band', 'patch'), may hold values from 0.3 to 3
- bad_lines: int32 [4, 256, 2], P('band', 'patch'), may hold values from 0 to 127
- destinations: int32 [4, 256, 1], P('band', 'patch'), may hold values from 0 to 7; in each aligned block of 32 rows (0 to 31, 32 to 63, ..., all dimensions but the last counted through in order) at most 8 rows name the same one
- tile_slots: int32 [4, 256], P('band', 'patch'), may hold values from 0 to 15
Outputs:
- coadd: float32 [4, 8, 256, 1024], P('band', 'patch')
- detection: float32 [8, 256, 1024], P('patch', 'band')
The draws below stay inside these ranges and needn't reach their ends.
Inputs may be any that keep to these rules, and one draw needn't show every extreme that they name: `destinations`: among the 32 pieces of one band held by one index of patch (aligned blocks), no patch is named more than 8 times, a bound that some block reaches.
All inputs are finite; a program needn't handle non-finite values.
Results may differ from the reference program's by a relative error of at most 0.00035.
Values sent between devices are 32-bit elements; how exact they have to be, the bound alone decides.
A program may use at most 192 MiB of HBM per device.

```python
import math
import jax
import jax.numpy as jnp
import numpy as np
from jax import lax

TILE = 128
RADIUS = 20
KERNELS = 3
TILES_X = 8
TILES_Y = 2
PIECES_DEV = 32
CAP = 8
BANDS = 4
PATCHES = 8
PIECES = 256


def set_ends(result, own_key, smallest, largest):
    longest = result.shape.index(max(result.shape))
    spots = []
    for shift in (0, 1):
        where = [jax.random.randint(jax.random.fold_in(own_key, axis), (), 0, length) for axis, length in enumerate(result.shape)]
        where[longest] = (where[longest] + shift) % result.shape[longest]
        spots.append(tuple(where))
    return result.at[spots[0]].set(smallest).at[spots[1]].set(largest)


def steps_of(rng, shape, shards, low, top_value):
    level, own = 1.0, jax.random.fold_in(rng, 6)
    for position, shards_of in shards:
        heights = jnp.exp(jax.random.uniform(jax.random.fold_in(own, position), (shards_of,), jnp.float32, low / len(shards), top_value / len(shards)))
        level = level * jnp.repeat(heights, shape[position] // shards_of).reshape([-1 if axis == position else 1 for axis in range(len(shape))])
    return level


def deal_out(stream_key, own, number, rows, count, top, bound, skew):
    ranking = jax.random.permutation(stream_key, count)
    crowded, ordinary = shares(count, rows * top, bound, skew, True), shares(count, rows * top, bound, skew, False)
    places = jnp.arange(count)

    def named(lengths, turn):
        used = int((lengths > 0).sum())
        fixed = max(1, used // 4)
        moved = fixed + (places - fixed + turn * (used - fixed)) % max(1, count - fixed)
        return jnp.zeros((count,), jnp.int32).at[ranking[jnp.where(places < fixed, places, moved)]].set(jnp.asarray(lengths, jnp.int32))

    lengths = jnp.where(number % 4 == 0, named(crowded, number // 4), named(ordinary, number - number // 4 - 1))
    mixed = jax.random.permutation(jax.random.fold_in(own, 3), count)
    giver, sink = mixed[0:count // 2 * 2:2], mixed[1:count // 2 * 2:2]
    room = jnp.minimum(lengths[giver] - 1, bound - lengths[sink]) // 2
    room = jnp.where((giver == ranking[0]) | (sink == ranking[0]) | (lengths[sink] == 0), 0, jnp.maximum(room, 0))
    moved = jax.random.randint(jax.random.fold_in(own, 4), (count // 2,), 0, 1 << 20) % (room + 1)
    lengths = lengths.at[giver].add(-moved).at[sink].add(moved)
    members = jnp.searchsorted(jnp.cumsum(lengths), jnp.arange(rows * top), side="right").astype(jnp.int32)
    table = members.reshape(top, rows).T
    table = table[jax.random.permutation(jax.random.fold_in(own, 1), rows)]
    turn = jax.random.randint(jax.random.fold_in(own, 2), (rows, 1), 0, top)
    return jnp.take_along_axis(table, (jnp.arange(top)[None, :] + turn) % top, axis=1)


def shares(number_of, total, bound, lean, full):
    weights = [(1 << 20) // math.isqrt(rank ** lean) + 1 for rank in range(1, number_of + 1)]
    largest = bound if full else min(bound, max(-(-total // number_of), total * weights[0] // sum(weights)))
    least = 1 if total - largest >= number_of - 1 else 0
    holding, rest = [largest] + [least] * (number_of - 1), total - largest - least * (number_of - 1)
    while rest > 0:
        free = [i for i in range(1, number_of) if holding[i] < largest] or [i for i in range(1, number_of) if holding[i] < bound]
        mass, budget = sum([weights[i] for i in free]), rest
        for i in free:
            more = min(bound - holding[i], max(1, budget * weights[i] // mass), rest)
            holding[i] = holding[i] + more
            rest = rest - more
    return np.array(holding)


def normal_values(rng, extent, width, reach, cuts=(), held_as=jnp.bfloat16):
    result = jax.random.normal(rng, extent, jnp.float32) * width
    if len(cuts) > 0:
        result = steps_of(rng, extent, cuts, -0.22, 0.18) * result
    return jnp.clip(result, min=-reach, max=reach).astype(held_as)


def setup_inputs(seed: int = 0) -> dict:
    key_list = jax.random.split(jax.random.key(seed), 7)
    images = normal_values(key_list[0], (BANDS, PIECES, TILE + 2 * RADIUS, TILE + 2 * RADIUS), 8.0, 48.0, ((0, 4), (1, 8)), jnp.float32)
    coeffs = jnp.clip(0.29882812 + 1.2011719 * jax.random.uniform(key_list[1], (BANDS, PIECES, KERNELS, TILE, TILE), jnp.float32) ** steps_of(key_list[1], (BANDS, PIECES, KERNELS, TILE, TILE), ((0, 4), (1, 8)), -0.2, 0.2), 0.29882812, 1.5).astype(jnp.bfloat16)
    inverse_var = jnp.clip(jnp.exp(math.log(3.0) - 2.3025851 * jax.random.uniform(key_list[2], (BANDS, PIECES, TILE, TILE), jnp.float32) ** steps_of(key_list[2], (BANDS, PIECES, TILE, TILE), ((0, 4), (1, 8)), -0.2, 0.2)), 0.3, 3.0)
    bad_lines = set_ends(jax.random.randint(key_list[3], (BANDS, PIECES, 2), 0, TILE), jax.random.fold_in(key_list[3], 1), 0, TILE - 1).astype(jnp.int32)
    destinations_keys = jax.random.split(jax.random.fold_in(key_list[4], 1), BANDS * PIECES // PIECES_DEV)
    destinations_turns = jax.random.permutation(jax.random.fold_in(key_list[4], 3), BANDS * PIECES // PIECES_DEV)
    destinations = jax.vmap(lambda own, number: deal_out(jax.random.fold_in(key_list[4], 2), own, number, PIECES_DEV, PATCHES, 1, CAP, 2))(destinations_keys, destinations_turns).reshape((BANDS, PIECES, 1))
    tile_slots = set_ends(jax.random.randint(key_list[5], (BANDS, PIECES), 0, TILES_X * TILES_Y), jax.random.fold_in(key_list[5], 1), 0, (TILES_X * TILES_Y) - 1).astype(jnp.int32)
    return {"images": images, "coeffs": coeffs, "inverse_var": inverse_var, "bad_lines": bad_lines, "destinations": destinations, "tile_slots": tile_slots}


HIGHEST = lax.Precision.HIGHEST
FRACTIONS = (0.12, 0.25, 0.45)
FLOOR = 0.5


def kernel_bands(tile_side, half_taps):
    offset = jnp.arange(tile_side + 2 * half_taps, dtype=jnp.int32)[None, :] - jnp.arange(tile_side, dtype=jnp.int32)[:, None]
    inside = (offset >= 0) & (offset <= 2 * half_taps)
    centred = (offset - half_taps).astype(jnp.float32)
    tap_offsets = (jnp.arange(2 * half_taps + 1, dtype=jnp.int32) - half_taps).astype(jnp.float32)
    matrices = []
    for fraction in FRACTIONS:
        sigma_width = fraction * half_taps
        tap_total = jnp.sum(jnp.exp(-0.5 * (tap_offsets / sigma_width) ** 2))
        matrices.append(jnp.where(inside, jnp.exp(-0.5 * (centred / sigma_width) ** 2) / tap_total, 0.0))
    return jnp.stack(matrices)


def match_pieces(images, coeffs, bands):
    rows_done = jnp.einsum("kyi,pij->pkyj", bands, images, precision=HIGHEST)
    smoothed = jnp.einsum("pkyj,kxj->pkyx", rows_done, bands, precision=HIGHEST)
    return jnp.sum(coeffs * smoothed, axis=1)


def reference(images, coeffs, inverse_var, bad_lines, destinations, tile_slots):
    bands = kernel_bands(TILE, RADIUS)
    line_index = jnp.arange(TILE, dtype=jnp.int32)
    tiles_all = TILES_Y * TILES_X
    coadd_list = []
    detection = jnp.zeros((PATCHES, TILES_Y * TILE, TILES_X * TILE), jnp.float32)
    for band_index in range(BANDS):
        matched = match_pieces(images[band_index], coeffs[band_index].astype(jnp.float32), bands)
        lines = bad_lines[band_index]
        keep_pixel = (line_index[None, :, None] != lines[:, 0][:, None, None]) & (line_index[None, None, :] != lines[:, 1][:, None, None])
        weight = jnp.where(keep_pixel, inverse_var[band_index], 0.0)
        segment_ids = (destinations[band_index, :, 0] * tiles_all + tile_slots[band_index]).astype(jnp.int32)
        numer_tiles = jax.ops.segment_sum(weight * matched, segment_ids, num_segments=PATCHES * tiles_all)
        denom_tiles = jax.ops.segment_sum(weight, segment_ids, num_segments=PATCHES * tiles_all)

        def assemble(planes):
            return planes.reshape(PATCHES, TILES_Y, TILES_X, TILE, TILE).transpose(0, 1, 3, 2, 4).reshape(PATCHES, TILES_Y * TILE, TILES_X * TILE)

        numerator = assemble(numer_tiles)
        denominator = assemble(denom_tiles)
        coadd = numerator / jnp.maximum(denominator, FLOOR)
        coadd_list.append(coadd)
        detection = detection + numerator * coadd
    return jnp.stack(coadd_list), detection
```

```python
import jax
import jax.numpy as jnp
from jax import lax
from jax.experimental import pallas as pl
from jax.experimental.pallas import tpu as pltpu
from jax.sharding import PartitionSpec as P

TILES_X = 8
TILES_Y = 2


HIGHEST = lax.Precision.HIGHEST
FRACTIONS = (0.12, 0.25, 0.45)
FLOOR = 0.5


def kernel_bands(tile_side, half_taps):
    offset = (
        jnp.arange(tile_side + 2 * half_taps, dtype=jnp.int32)[None, :]
        - jnp.arange(tile_side, dtype=jnp.int32)[:, None]
    )
    inside = (offset >= 0) & (offset <= 2 * half_taps)
    centred = (offset - half_taps).astype(jnp.float32)
    tap_offsets = (jnp.arange(2 * half_taps + 1, dtype=jnp.int32) - half_taps).astype(jnp.float32)
    matrices = []
    for fraction in FRACTIONS:
        sigma_width = fraction * half_taps
        tap_total = jnp.sum(jnp.exp(-0.5 * (tap_offsets / sigma_width) ** 2))
        matrices.append(
            jnp.where(inside, jnp.exp(-0.5 * (centred / sigma_width) ** 2) / tap_total, 0.0)
        )
    return jnp.stack(matrices)


def match_pieces(images, coeffs, bands):
    rows_done = jnp.einsum("kyi,pij->pkyj", bands, images, precision=HIGHEST)
    smoothed = jnp.einsum("pkyj,kxj->pkyx", rows_done, bands, precision=HIGHEST)
    return jnp.sum(coeffs * smoothed, axis=1)


def slot_matrix(targets, tile_index, owners_count, slot_depth):
    owners = jnp.arange(owners_count, dtype=jnp.int32)
    onehot = (targets[:, None] == owners[None, :]).astype(jnp.int32)
    before = jnp.cumsum(onehot, axis=0) - onehot
    slot_rank = jnp.sum(before * onehot, axis=1)
    slot_index = targets * slot_depth + slot_rank
    slot_range = jnp.arange(owners_count * slot_depth, dtype=jnp.int32)
    chosen = slot_range[:, None] == slot_index[None, :]
    selector = chosen.astype(jnp.float32)
    position = jnp.sum(jnp.where(chosen, tile_index[None, :] + 1, 0), axis=1) - 1
    return (selector, position.astype(jnp.float32).reshape(owners_count, slot_depth))


def pack_slots(selector, slot_data, owners_count, slot_depth):
    flat_rows = slot_data.reshape(slot_data.shape[0], -1)
    packed = jnp.dot(selector, flat_rows, precision=HIGHEST, preferred_element_type=jnp.float32)
    return packed.reshape((owners_count, slot_depth) + slot_data.shape[1:])


def exchanged_raw(images, coeffs, inverse_var, bad_lines, destinations, tile_slots):
    owners_count = lax.axis_size("patch")
    piece_count = images.shape[1]
    slot_depth = max(2, 2 * piece_count // owners_count)
    tile_side = inverse_var.shape[-1]
    half_taps = (images.shape[-1] - tile_side) // 2
    bands = kernel_bands(tile_side, half_taps)
    line_index = jnp.arange(tile_side, dtype=jnp.int32)
    lines = bad_lines[0]
    keep_pixel = (line_index[None, :, None] != lines[:, 0][:, None, None]) & (
        line_index[None, None, :] != lines[:, 1][:, None, None]
    )
    weight = jnp.where(keep_pixel, inverse_var[0], 0.0)
    selector, position = slot_matrix(destinations[0, :, 0], tile_slots[0], owners_count, slot_depth)
    raw_slots = pack_slots(selector, images[0], owners_count, slot_depth)
    coeff_slots = pack_slots(selector, coeffs[0].astype(jnp.float32), owners_count, slot_depth)
    weight_slots = pack_slots(selector, weight, owners_count, slot_depth)
    image_part = lax.all_to_all(raw_slots, "patch", split_axis=0, concat_axis=0, tiled=True)
    coeff_part = lax.all_to_all(coeff_slots, "patch", split_axis=0, concat_axis=0, tiled=True)
    weight_part = lax.all_to_all(weight_slots, "patch", split_axis=0, concat_axis=0, tiled=True)
    place_part = lax.all_to_all(position, "patch", split_axis=0, concat_axis=0, tiled=True)
    lead_shape = image_part.shape[:2]
    matched = match_pieces(
        image_part.reshape((-1,) + image_part.shape[2:]),
        coeff_part.reshape((-1,) + coeff_part.shape[2:]),
        bands,
    )
    matched = matched.reshape(lead_shape + (tile_side, tile_side))
    numer_slots = weight_part * matched
    flat_places = place_part.reshape(-1)
    tile_targets = jnp.arange(TILES_Y * TILES_X, dtype=jnp.float32)
    spread = (tile_targets[:, None] == flat_places[None, :]).astype(jnp.float32)

    def assemble(planes):
        summed = jnp.dot(
            spread,
            planes.reshape(flat_places.shape[0], -1),
            precision=HIGHEST,
            preferred_element_type=jnp.float32,
        )
        return (
            summed.reshape(TILES_Y, TILES_X, tile_side, tile_side)
            .transpose(0, 2, 1, 3)
            .reshape(TILES_Y * tile_side, TILES_X * tile_side)
        )

    numerator = assemble(numer_slots)
    denominator = assemble(weight_part)
    coadd = numerator / jnp.maximum(denominator, FLOOR)
    detection = lax.psum_scatter(numerator * coadd, "band", scatter_dimension=0, tiled=True)
    return (coadd[None, None], detection[None])


TILES = TILES_Y * TILES_X
GROUP = 4
CHUNKS = 8
MESH = pl.DeviceIdType.MESH


def split(value):
    high = value.astype(jnp.bfloat16)
    return high, (value - high.astype(jnp.float32)).astype(jnp.bfloat16)


def dot(a, b):
    return jnp.dot(a, b, preferred_element_type=jnp.float32)


def match_kernel(lines_ref, image_ref, coeff_ref, var_ref, rows_ref, cols_ref, out_ref):
    step = pl.program_id(0)
    side = var_ref.shape[-1]
    count = out_ref.shape[0] // (2 * side)
    row = lax.broadcasted_iota(jnp.int32, (side, side), 0)
    col = lax.broadcasted_iota(jnp.int32, (side, side), 1)
    for i in range(GROUP):
        piece = step * GROUP + i
        high, low = split(image_ref[i])
        done = dot(rows_ref[0], high) + dot(rows_ref[0], low) + dot(rows_ref[1], high)
        high, low = split(done)
        matched = None
        for k in range(coeff_ref.shape[1]):
            ys = slice(k * side, (k + 1) * side)
            both = dot(high[ys], cols_ref[k])
            smooth = both[:, :side] + both[:, side:] + dot(low[ys], cols_ref[k, :, :side])
            term = coeff_ref[i, k].astype(jnp.float32) * smooth
            matched = term if matched is None else matched + term
        masked = (row == lines_ref[piece, 0]) | (col == lines_ref[piece, 1])
        weight = jnp.where(masked, 0.0, var_ref[i])
        out_ref[pl.ds(piece, side, stride=2 * count), :] = weight * matched
        out_ref[pl.ds(count + piece, side, stride=2 * count), :] = weight


def match_local(images, coeffs, inverse_var, lines, bands):
    count, wide, _ = images.shape
    kernels, side, _ = bands.shape
    rounded = lax.reduce_precision(bands, 8, 7)
    high, low = rounded.astype(jnp.bfloat16), (bands - rounded).astype(jnp.bfloat16)
    rows = jnp.stack([high.reshape(kernels * side, wide), low.reshape(kernels * side, wide)])
    cols = jnp.concatenate([jnp.swapaxes(high, 1, 2), jnp.swapaxes(low, 1, 2)], axis=2)
    out = pl.pallas_call(
        match_kernel,
        out_shape=jax.ShapeDtypeStruct((side * 2 * count, side), jnp.float32),
        grid_spec=pltpu.PrefetchScalarGridSpec(
            num_scalar_prefetch=1,
            grid=(count // GROUP,),
            in_specs=[
                pl.BlockSpec((GROUP, wide, wide), lambda i, _: (i, 0, 0)),
                pl.BlockSpec((GROUP, kernels, side, side), lambda i, _: (i, 0, 0, 0)),
                pl.BlockSpec((GROUP, side, side), lambda i, _: (i, 0, 0)),
                pl.BlockSpec(rows.shape, lambda i, _: (0, 0, 0)),
                pl.BlockSpec(cols.shape, lambda i, _: (0, 0, 0)),
            ],
            out_specs=pl.BlockSpec((side * 2 * count, side), lambda i, _: (0, 0)),
        ),
        compiler_params=pltpu.CompilerParams(vmem_limit_bytes=48 * 1024 * 1024),
        cost_estimate=pl.CostEstimate(
            flops=count * 36 * kernels * side * wide * side, bytes_accessed=14 << 20, transcendentals=0
        ),
    )(lines, images, coeffs, inverse_var, rows, cols)
    return out.reshape(side, 2, count, side)


def line_kernel(
    data, pick, total,
    units, listed, summed, to_across, to_outer, from_inner, own_sum, to_sib, from_sib,
    local_sem, share_send, share_recv, list_send, list_recv, across_send, across_recv,
    outer_send, outer_recv, final_send, final_recv,
):
    me = lax.axis_index("patch")
    z, core = me // 2, me % 2
    half_rows = units.shape[0]
    step_rows = half_rows // CHUNKS
    side = z // 2
    is_outer = (z == 0) | (z == 3)
    is_inner = (z == 1) | (z == 2)
    sibling = {"patch": z * 2 + 1 - core}
    inward = {"patch": (1 + side) * 2 + core}
    outward = {"patch": 3 * side * 2 + core}
    across = {"patch": (2 - side) * 2 + core}
    pieces = data.shape[2]

    barrier = pltpu.get_barrier_semaphore()
    pl.semaphore_signal(barrier, inc=1, device_id=sibling, device_id_type=MESH)

    @pl.when(is_outer)
    def _():
        pl.semaphore_signal(barrier, inc=1, device_id=inward, device_id_type=MESH)
        pl.semaphore_wait(barrier, 2)

    @pl.when(is_inner)
    def _():
        pl.semaphore_signal(barrier, inc=1, device_id=outward, device_id_type=MESH)
        pl.semaphore_signal(barrier, inc=1, device_id=across, device_id_type=MESH)
        pl.semaphore_wait(barrier, 3)

    def rows_of(i):
        return pl.ds(i * step_rows, step_rows)

    def remote(source, target, send, recv, device):
        return pltpu.make_async_remote_copy(
            src_ref=source, dst_ref=target, send_sem=send, recv_sem=recv,
            device_id=device, device_id_type=MESH,
        )

    def share(i):
        return remote(
            data.at[pl.ds((1 - core) * half_rows + i * step_rows, step_rows)],
            units.at[rows_of(i), :, pl.ds(pieces, pieces)],
            share_send.at[i], share_recv.at[i], sibling,
        )

    def send_list(i):
        return remote(units.at[rows_of(i)], listed.at[rows_of(i)], list_send.at[i], list_recv.at[i], inward)

    def send_across(i):
        return remote(to_across.at[rows_of(i)], summed.at[rows_of(i)], across_send.at[i], across_recv.at[i], across)

    def send_outer(i):
        return remote(to_outer.at[rows_of(i)], from_inner.at[rows_of(i)], outer_send.at[i], outer_recv.at[i], outward)

    def send_final(i):
        return remote(to_sib.at[rows_of(i)], from_sib.at[rows_of(i)], final_send.at[i], final_recv.at[i], sibling)

    own_copy = pltpu.make_async_copy(
        data.at[pl.ds(core * half_rows, half_rows)], units.at[:, :, pl.ds(0, pieces)], local_sem
    )
    own_copy.start()

    @pl.loop(0, CHUNKS)
    def _(i):
        share(i).start()

    own_copy.wait()

    def placed(y, row_from, with_list):
        parts = []
        for q in range(2):
            value = units[y, q]
            if with_list:
                value = jnp.concatenate([value, listed[y, q]], axis=0)
            parts.append(value)
        high, low = split(jnp.concatenate(parts, axis=1))
        both = jnp.concatenate([high, low], axis=0)
        wide = pick.shape[1] // 2
        if with_list:
            chosen = pick[pl.ds(row_from, pick.shape[0] - row_from), :]
        else:
            chosen = pick[pl.ds(row_from, pick.shape[0] - row_from), pl.ds(0, wide)]
        return dot(chosen, both)

    def finish(y, extra):
        for q in range(2):
            value = own_sum[y, q] + extra[y, q, -32:]
            total[core * half_rows + y, q] = value[:TILES]
            to_sib[y, q] = value[TILES:]

    @pl.when(is_outer)
    def _():
        @pl.loop(0, CHUNKS + 2)
        def _(i):
            @pl.when(i < CHUNKS)
            def _():
                share(i).wait_recv()
                send_list(i).start()

                @pl.loop(0, step_rows)
                def _(r):
                    y = i * step_rows + r
                    value = placed(y, 6 * TILES, False)
                    lanes = value.shape[1] // 2
                    for q in range(2):
                        own_sum[y, q] = value[:, q * lanes:(q + 1) * lanes]

            @pl.when(i >= 2)
            def _():
                j = i - 2
                send_outer(j).wait_recv()

                @pl.loop(0, step_rows)
                def _(r):
                    finish(j * step_rows + r, from_inner)

                send_final(j).start()

        @pl.loop(0, CHUNKS)
        def _(i):
            send_list(i).wait_send()

    @pl.when(is_inner)
    def _():
        @pl.loop(0, CHUNKS + 2)
        def _(i):
            @pl.when(i < CHUNKS)
            def _():
                share(i).wait_recv()
                send_list(i).wait_recv()

                @pl.loop(0, step_rows)
                def _(r):
                    y = i * step_rows + r
                    value = placed(y, 0, True)
                    lanes = value.shape[1] // 2
                    for q in range(2):
                        here = value[:, q * lanes:(q + 1) * lanes]
                        to_across[y, q] = here[:4 * TILES]
                        to_outer[y, q] = here[4 * TILES:6 * TILES]
                        own_sum[y, q] = here[6 * TILES:]

                send_across(i).start()

            @pl.when(i >= 2)
            def _():
                j = i - 2
                send_across(j).wait_recv()

                @pl.loop(0, step_rows)
                def _(r):
                    y = j * step_rows + r
                    for q in range(2):
                        to_outer[y, q] = to_outer[y, q] + summed[y, q, :2 * TILES]
                    finish(y, summed)

                send_outer(j).start()
                send_final(j).start()

        @pl.loop(0, CHUNKS)
        def _(i):
            send_across(i).wait_send()
            send_outer(i).wait_send()

    @pl.loop(0, CHUNKS)
    def _(i):
        share(i).wait_send()
        send_final(i).wait()

        @pl.loop(0, step_rows)
        def _(r):
            y = i * step_rows + r
            total[(1 - core) * half_rows + y] = from_sib[y]


def exchange_line(data, labels):
    side, _, pieces, lanes = data.shape
    half_rows = side // 2
    me = lax.axis_index("patch")
    z, core = me // 2, me % 2
    near = z // 2
    inner = (z == 1) | (z == 2)
    everyone = lax.all_gather(labels, "patch", axis=0, tiled=False)
    pair = jnp.stack([core, 1 - core])
    chips = jnp.stack([3 * (1 - near), 2 - near, 3 * near, z])
    order = (chips[:, None] * 2 + pair[None, :]).reshape(-1)
    wanted = (order[:, None] * TILES + jnp.arange(TILES)[None, :]).reshape(-1)
    mine = everyone[z * 2 + pair].reshape(-1)
    theirs = everyone[3 * near * 2 + pair].reshape(-1)
    of_mine = wanted[:, None] == mine[None, :]
    to_outer = (jnp.arange(8 * TILES) // (2 * TILES)) == 2
    of_theirs = (wanted[:, None] == theirs[None, :]) & ~to_outer[:, None]
    inner_pick = jnp.concatenate([of_mine, of_theirs, of_mine, of_theirs], axis=1)
    outer_pick = jnp.concatenate([of_mine, of_mine, of_mine, of_mine], axis=1)
    pick = jnp.where(inner, inner_pick, outer_pick).astype(jnp.bfloat16)

    def plane(count):
        return pltpu.VMEM((half_rows, 2, count, lanes), jnp.float32)

    many = pltpu.SemaphoreType.DMA((CHUNKS,))
    return pl.pallas_call(
        line_kernel,
        out_shape=jax.ShapeDtypeStruct((side, 2, TILES, lanes), jnp.float32),
        in_specs=[pl.BlockSpec(memory_space=pl.ANY), pl.BlockSpec(memory_space=pltpu.VMEM)],
        out_specs=pl.BlockSpec(memory_space=pltpu.VMEM),
        scratch_shapes=[
            plane(2 * pieces), plane(2 * pieces), plane(4 * TILES), plane(4 * TILES),
            plane(2 * TILES), plane(2 * TILES), plane(2 * TILES), plane(TILES), plane(TILES),
            pltpu.SemaphoreType.DMA,
        ] + [many] * 10,
        compiler_params=pltpu.CompilerParams(
            collective_id=0, has_side_effects=True, vmem_limit_bytes=48 * 1024 * 1024
        ),
        cost_estimate=pl.CostEstimate(flops=4 << 30, bytes_accessed=300 << 20, transcendentals=0),
    )(data, pick)


def coadd_kernel(total_ref, coadd_ref, term_ref):
    side = total_ref.shape[1]
    for ty in range(TILES_Y):
        for tx in range(TILES_X):
            tile = ty * TILES_X + tx
            numer = total_ref[pl.ds(tile, side, stride=2 * TILES), :]
            denom = total_ref[pl.ds(TILES + tile, side, stride=2 * TILES), :]
            coadd = numer / jnp.maximum(denom, FLOOR)
            spot = (slice(ty * side, (ty + 1) * side), slice(tx * side, (tx + 1) * side))
            coadd_ref[spot] = coadd
            term_ref[spot] = numer * coadd


def per_device(images, coeffs, inverse_var, bad_lines, destinations, tile_slots):
    owners_count = lax.axis_size("patch")
    piece_count = images.shape[1]
    if owners_count != 8 or piece_count != 32:
        return exchanged_raw(images, coeffs, inverse_var, bad_lines, destinations, tile_slots)
    tile_side = inverse_var.shape[-1]
    half_taps = (images.shape[-1] - tile_side) // 2
    bands = kernel_bands(tile_side, half_taps)
    labels = destinations[0, :, 0] * TILES + tile_slots[0]
    data = match_local(images[0], coeffs[0], inverse_var[0], bad_lines[0], bands)
    total = exchange_line(data, labels)
    shape = jax.ShapeDtypeStruct((TILES_Y * tile_side, TILES_X * tile_side), jnp.float32)
    coadd, terms = pl.pallas_call(
        coadd_kernel,
        out_shape=(shape, shape),
        compiler_params=pltpu.CompilerParams(vmem_limit_bytes=32 * 1024 * 1024),
    )(total.reshape(-1, tile_side))
    detection = lax.psum_scatter(terms, "band", scatter_dimension=0, tiled=True)
    return (coadd[None, None], detection[None])


def solution(mesh):
    in_specs = (
        P("band", "patch", None, None),
        P("band", "patch", None, None, None),
        P("band", "patch", None, None),
        P("band", "patch", None),
        P("band", "patch", None),
        P("band", "patch"),
    )
    out_specs = (P("band", "patch", None, None), P("patch", "band", None))
    return jax.shard_map(
        per_device, mesh=mesh, in_specs=in_specs, out_specs=out_specs, check_vma=False
    )
```

```python
import jax
import jax.numpy as jnp
import numpy as np
from jax import lax
from jax.experimental import pallas as pl
from jax.experimental.pallas import tpu as pltpu
from jax.sharding import PartitionSpec as P

TILES_X = 8
TILES_Y = 2


HIGHEST = lax.Precision.HIGHEST
FRACTIONS = (0.12, 0.25, 0.45)
FLOOR = 0.5


def kernel_bands(tile_side, half_taps):
    offset = (
        jnp.arange(tile_side + 2 * half_taps, dtype=jnp.int32)[None, :]
        - jnp.arange(tile_side, dtype=jnp.int32)[:, None]
    )
    inside = (offset >= 0) & (offset <= 2 * half_taps)
    centred = (offset - half_taps).astype(jnp.float32)
    tap_offsets = (jnp.arange(2 * half_taps + 1, dtype=jnp.int32) - half_taps).astype(jnp.float32)
    matrices = []
    for fraction in FRACTIONS:
        sigma_width = fraction * half_taps
        tap_total = jnp.sum(jnp.exp(-0.5 * (tap_offsets / sigma_width) ** 2))
        matrices.append(
            jnp.where(inside, jnp.exp(-0.5 * (centred / sigma_width) ** 2) / tap_total, 0.0)
        )
    return jnp.stack(matrices)


def match_pieces(images, coeffs, bands):
    rows_done = jnp.einsum("kyi,pij->pkyj", bands, images, precision=HIGHEST)
    smoothed = jnp.einsum("pkyj,kxj->pkyx", rows_done, bands, precision=HIGHEST)
    return jnp.sum(coeffs * smoothed, axis=1)


def slot_matrix(targets, tile_index, owners_count, slot_depth):
    owners = jnp.arange(owners_count, dtype=jnp.int32)
    onehot = (targets[:, None] == owners[None, :]).astype(jnp.int32)
    before = jnp.cumsum(onehot, axis=0) - onehot
    slot_rank = jnp.sum(before * onehot, axis=1)
    slot_index = targets * slot_depth + slot_rank
    slot_range = jnp.arange(owners_count * slot_depth, dtype=jnp.int32)
    chosen = slot_range[:, None] == slot_index[None, :]
    selector = chosen.astype(jnp.float32)
    position = jnp.sum(jnp.where(chosen, tile_index[None, :] + 1, 0), axis=1) - 1
    return (selector, position.astype(jnp.float32).reshape(owners_count, slot_depth))


def pack_slots(selector, slot_data, owners_count, slot_depth):
    flat_rows = slot_data.reshape(slot_data.shape[0], -1)
    packed = jnp.dot(selector, flat_rows, precision=HIGHEST, preferred_element_type=jnp.float32)
    return packed.reshape((owners_count, slot_depth) + slot_data.shape[1:])


def exchanged_raw(images, coeffs, inverse_var, bad_lines, destinations, tile_slots):
    owners_count = lax.axis_size("patch")
    piece_count = images.shape[1]
    slot_depth = max(2, 2 * piece_count // owners_count)
    tile_side = inverse_var.shape[-1]
    half_taps = (images.shape[-1] - tile_side) // 2
    bands = kernel_bands(tile_side, half_taps)
    line_index = jnp.arange(tile_side, dtype=jnp.int32)
    lines = bad_lines[0]
    keep_pixel = (line_index[None, :, None] != lines[:, 0][:, None, None]) & (
        line_index[None, None, :] != lines[:, 1][:, None, None]
    )
    weight = jnp.where(keep_pixel, inverse_var[0], 0.0)
    selector, position = slot_matrix(destinations[0, :, 0], tile_slots[0], owners_count, slot_depth)
    raw_slots = pack_slots(selector, images[0], owners_count, slot_depth)
    coeff_slots = pack_slots(selector, coeffs[0].astype(jnp.float32), owners_count, slot_depth)
    weight_slots = pack_slots(selector, weight, owners_count, slot_depth)
    image_part = lax.all_to_all(raw_slots, "patch", split_axis=0, concat_axis=0, tiled=True)
    coeff_part = lax.all_to_all(coeff_slots, "patch", split_axis=0, concat_axis=0, tiled=True)
    weight_part = lax.all_to_all(weight_slots, "patch", split_axis=0, concat_axis=0, tiled=True)
    place_part = lax.all_to_all(position, "patch", split_axis=0, concat_axis=0, tiled=True)
    lead_shape = image_part.shape[:2]
    matched = match_pieces(
        image_part.reshape((-1,) + image_part.shape[2:]),
        coeff_part.reshape((-1,) + coeff_part.shape[2:]),
        bands,
    )
    matched = matched.reshape(lead_shape + (tile_side, tile_side))
    numer_slots = weight_part * matched
    flat_places = place_part.reshape(-1)
    tile_targets = jnp.arange(TILES_Y * TILES_X, dtype=jnp.float32)
    spread = (tile_targets[:, None] == flat_places[None, :]).astype(jnp.float32)

    def assemble(planes):
        summed = jnp.dot(
            spread,
            planes.reshape(flat_places.shape[0], -1),
            precision=HIGHEST,
            preferred_element_type=jnp.float32,
        )
        return (
            summed.reshape(TILES_Y, TILES_X, tile_side, tile_side)
            .transpose(0, 2, 1, 3)
            .reshape(TILES_Y * tile_side, TILES_X * tile_side)
        )

    numerator = assemble(numer_slots)
    denominator = assemble(weight_part)
    coadd = numerator / jnp.maximum(denominator, FLOOR)
    detection = lax.psum_scatter(numerator * coadd, "band", scatter_dimension=0, tiled=True)
    return (coadd[None, None], detection[None])


TILES = TILES_Y * TILES_X
GROUP = 4
CHUNKS = 16
MESH = pl.DeviceIdType.MESH


def split(value):
    high = value.astype(jnp.bfloat16)
    return high, (value - high.astype(jnp.float32)).astype(jnp.bfloat16)


def dot(a, b):
    return jnp.dot(a, b, preferred_element_type=jnp.float32)


def match_kernel(lines_ref, image_ref, coeff_ref, var_ref, rows_ref, cols_ref, out_ref):
    step = pl.program_id(0)
    side = var_ref.shape[-1]
    count = out_ref.shape[0] // (2 * side)
    row = lax.broadcasted_iota(jnp.int32, (side, side), 0)
    col = lax.broadcasted_iota(jnp.int32, (side, side), 1)
    for i in range(GROUP):
        piece = step * GROUP + i
        high, low = split(image_ref[i])
        done = dot(rows_ref[0], high) + dot(rows_ref[0], low) + dot(rows_ref[1], high)
        high, low = split(done)
        matched = None
        for k in range(coeff_ref.shape[1]):
            ys = slice(k * side, (k + 1) * side)
            both = dot(high[ys], cols_ref[k])
            smooth = both[:, :side] + both[:, side:] + dot(low[ys], cols_ref[k, :, :side])
            term = coeff_ref[i, k].astype(jnp.float32) * smooth
            matched = term if matched is None else matched + term
        masked = (row == lines_ref[piece, 0]) | (col == lines_ref[piece, 1])
        weight = jnp.where(masked, 0.0, var_ref[i])
        out_ref[pl.ds(piece, side, stride=2 * count), :] = weight * matched
        out_ref[pl.ds(count + piece, side, stride=2 * count), :] = weight


def fixed_bands(tile_side, half_taps):
    offset = np.arange(tile_side + 2 * half_taps)[None, :] - np.arange(tile_side)[:, None]
    inside = (offset >= 0) & (offset <= 2 * half_taps)
    taps = np.arange(2 * half_taps + 1) - half_taps
    matrices = []
    for fraction in FRACTIONS:
        sigma = fraction * half_taps
        total = np.sum(np.exp(-0.5 * (taps / sigma) ** 2))
        matrices.append(np.where(inside, np.exp(-0.5 * ((offset - half_taps) / sigma) ** 2) / total, 0.0))
    return np.stack(matrices).astype(np.float32)


def match_local(images, coeffs, inverse_var, lines, bands):
    count, wide, _ = images.shape
    kernels, side, _ = bands.shape
    high = bands.astype(jnp.bfloat16)
    low = (bands - high.astype(np.float32)).astype(jnp.bfloat16)
    rows = jnp.asarray(np.stack([high.reshape(kernels * side, wide), low.reshape(kernels * side, wide)]))
    cols = jnp.asarray(np.concatenate([np.swapaxes(high, 1, 2), np.swapaxes(low, 1, 2)], axis=2))
    out = pl.pallas_call(
        match_kernel,
        out_shape=jax.ShapeDtypeStruct((side * 2 * count, side), jnp.float32),
        grid_spec=pltpu.PrefetchScalarGridSpec(
            num_scalar_prefetch=1,
            grid=(count // GROUP,),
            in_specs=[
                pl.BlockSpec((GROUP, wide, wide), lambda i, _: (i, 0, 0)),
                pl.BlockSpec((GROUP, kernels, side, side), lambda i, _: (i, 0, 0, 0)),
                pl.BlockSpec((GROUP, side, side), lambda i, _: (i, 0, 0)),
                pl.BlockSpec(rows.shape, lambda i, _: (0, 0, 0)),
                pl.BlockSpec(cols.shape, lambda i, _: (0, 0, 0)),
            ],
            out_specs=pl.BlockSpec((side * 2 * count, side), lambda i, _: (0, 0)),
        ),
        compiler_params=pltpu.CompilerParams(vmem_limit_bytes=48 * 1024 * 1024),
        cost_estimate=pl.CostEstimate(
            flops=count * 36 * kernels * side * wide * side, bytes_accessed=14 << 20, transcendentals=0
        ),
    )(lines, images, coeffs, inverse_var, rows, cols)
    return out.reshape(side, 2, count, side)


def line_kernel(
    data, pick, total,
    units, listed, summed, to_across, to_outer, from_inner, own_sum, to_sib, from_sib,
    local_sem, share_send, share_recv, list_send, list_recv, across_send, across_recv,
    outer_send, outer_recv, final_send, final_recv,
):
    me = lax.axis_index("patch")
    z, core = me // 2, me % 2
    half_rows = units.shape[0]
    step_rows = half_rows // CHUNKS
    side = z // 2
    is_outer = (z == 0) | (z == 3)
    is_inner = (z == 1) | (z == 2)
    sibling = {"patch": z * 2 + 1 - core}
    inward = {"patch": (1 + side) * 2 + core}
    outward = {"patch": 3 * side * 2 + core}
    across = {"patch": (2 - side) * 2 + core}
    pieces = data.shape[2]

    barrier = pltpu.get_barrier_semaphore()
    pl.semaphore_signal(barrier, inc=1, device_id=sibling, device_id_type=MESH)

    @pl.when(is_outer)
    def _():
        pl.semaphore_signal(barrier, inc=1, device_id=inward, device_id_type=MESH)
        pl.semaphore_wait(barrier, 2)

    @pl.when(is_inner)
    def _():
        pl.semaphore_signal(barrier, inc=1, device_id=outward, device_id_type=MESH)
        pl.semaphore_signal(barrier, inc=1, device_id=across, device_id_type=MESH)
        pl.semaphore_wait(barrier, 3)

    def rows_of(i):
        return pl.ds(i * step_rows, step_rows)

    def remote(source, target, send, recv, device):
        return pltpu.make_async_remote_copy(
            src_ref=source, dst_ref=target, send_sem=send, recv_sem=recv,
            device_id=device, device_id_type=MESH,
        )

    def share(i):
        return remote(
            data.at[pl.ds((1 - core) * half_rows + i * step_rows, step_rows)],
            units.at[rows_of(i), :, pl.ds(pieces, pieces)],
            share_send.at[i], share_recv.at[i], sibling,
        )

    def send_list(i):
        return remote(units.at[rows_of(i)], listed.at[rows_of(i)], list_send.at[i], list_recv.at[i], inward)

    def send_across(i):
        return remote(to_across.at[rows_of(i)], summed.at[rows_of(i)], across_send.at[i], across_recv.at[i], across)

    def send_outer(i):
        return remote(to_outer.at[rows_of(i)], from_inner.at[rows_of(i)], outer_send.at[i], outer_recv.at[i], outward)

    def send_final(i):
        return remote(to_sib.at[rows_of(i)], from_sib.at[rows_of(i)], final_send.at[i], final_recv.at[i], sibling)

    own_copy = pltpu.make_async_copy(
        data.at[pl.ds(core * half_rows, half_rows)], units.at[:, :, pl.ds(0, pieces)], local_sem
    )
    own_copy.start()

    @pl.loop(0, CHUNKS)
    def _(i):
        share(i).start()

    own_copy.wait()

    def placed(y, row_from, with_list):
        parts = []
        for q in range(2):
            value = units[y, q]
            if with_list:
                value = jnp.concatenate([value, listed[y, q]], axis=0)
            parts.append(value)
        high, low = split(jnp.concatenate(parts, axis=1))
        both = jnp.concatenate([high, low], axis=0)
        wide = pick.shape[1] // 2
        if with_list:
            chosen = pick[pl.ds(row_from, pick.shape[0] - row_from), :]
        else:
            chosen = pick[pl.ds(row_from, pick.shape[0] - row_from), pl.ds(0, wide)]
        return dot(chosen, both)

    def finish(y, extra):
        for q in range(2):
            value = own_sum[y, q] + extra[y, q, -32:]
            total[core * half_rows + y, q] = value[:TILES]
            to_sib[y, q] = value[TILES:]

    @pl.when(is_outer)
    def _():
        @pl.loop(0, CHUNKS + 2)
        def _(i):
            @pl.when(i < CHUNKS)
            def _():
                share(i).wait_recv()
                send_list(i).start()

                @pl.loop(0, step_rows)
                def _(r):
                    y = i * step_rows + r
                    value = placed(y, 6 * TILES, False)
                    lanes = value.shape[1] // 2
                    for q in range(2):
                        own_sum[y, q] = value[:, q * lanes:(q + 1) * lanes]

            @pl.when(i >= 2)
            def _():
                j = i - 2
                send_outer(j).wait_recv()

                @pl.loop(0, step_rows)
                def _(r):
                    finish(j * step_rows + r, from_inner)

                send_final(j).start()

        @pl.loop(0, CHUNKS)
        def _(i):
            send_list(i).wait_send()

    @pl.when(is_inner)
    def _():
        @pl.loop(0, CHUNKS + 2)
        def _(i):
            @pl.when(i < CHUNKS)
            def _():
                share(i).wait_recv()
                send_list(i).wait_recv()

                @pl.loop(0, step_rows)
                def _(r):
                    y = i * step_rows + r
                    value = placed(y, 0, True)
                    lanes = value.shape[1] // 2
                    for q in range(2):
                        here = value[:, q * lanes:(q + 1) * lanes]
                        to_across[y, q] = here[:4 * TILES]
                        to_outer[y, q] = here[4 * TILES:6 * TILES]
                        own_sum[y, q] = here[6 * TILES:]

                send_across(i).start()

            @pl.when(i >= 2)
            def _():
                j = i - 2
                send_across(j).wait_recv()

                @pl.loop(0, step_rows)
                def _(r):
                    y = j * step_rows + r
                    for q in range(2):
                        to_outer[y, q] = to_outer[y, q] + summed[y, q, :2 * TILES]
                    finish(y, summed)

                send_outer(j).start()
                send_final(j).start()

        @pl.loop(0, CHUNKS)
        def _(i):
            send_across(i).wait_send()
            send_outer(i).wait_send()

    @pl.loop(0, CHUNKS)
    def _(i):
        share(i).wait_send()
        send_final(i).wait()

        @pl.loop(0, step_rows)
        def _(r):
            y = i * step_rows + r
            total[(1 - core) * half_rows + y] = from_sib[y]


def exchange_line(data, labels):
    side, _, pieces, lanes = data.shape
    half_rows = side // 2
    me = lax.axis_index("patch")
    z, core = me // 2, me % 2
    near = z // 2
    inner = (z == 1) | (z == 2)
    others = [
        lax.ppermute(labels, "patch", [(p, p ^ turn) for p in range(lax.axis_size("patch"))])
        for turn in (1, 2, 3)
    ]
    pair = jnp.stack([core, 1 - core])
    chips = jnp.stack([3 * (1 - near), 2 - near, 3 * near, z])
    order = (chips[:, None] * 2 + pair[None, :]).reshape(-1)
    wanted = (order[:, None] * TILES + jnp.arange(TILES)[None, :]).reshape(-1)
    mine = jnp.concatenate([labels, others[0]])
    theirs = jnp.concatenate([others[1], others[2]])
    of_mine = wanted[:, None] == mine[None, :]
    to_outer = (jnp.arange(8 * TILES) // (2 * TILES)) == 2
    of_theirs = (wanted[:, None] == theirs[None, :]) & ~to_outer[:, None]
    inner_pick = jnp.concatenate([of_mine, of_theirs, of_mine, of_theirs], axis=1)
    outer_pick = jnp.concatenate([of_mine, of_mine, of_mine, of_mine], axis=1)
    pick = jnp.where(inner, inner_pick, outer_pick).astype(jnp.bfloat16)

    def plane(count):
        return pltpu.VMEM((half_rows, 2, count, lanes), jnp.float32)

    many = pltpu.SemaphoreType.DMA((CHUNKS,))
    return pl.pallas_call(
        line_kernel,
        out_shape=jax.ShapeDtypeStruct((side, 2, TILES, lanes), jnp.float32),
        in_specs=[pl.BlockSpec(memory_space=pl.ANY), pl.BlockSpec(memory_space=pltpu.VMEM)],
        out_specs=pl.BlockSpec(memory_space=pltpu.VMEM),
        scratch_shapes=[
            plane(2 * pieces), plane(2 * pieces), plane(4 * TILES), plane(4 * TILES),
            plane(2 * TILES), plane(2 * TILES), plane(2 * TILES), plane(TILES), plane(TILES),
            pltpu.SemaphoreType.DMA,
        ] + [many] * 10,
        compiler_params=pltpu.CompilerParams(
            collective_id=0, has_side_effects=True, vmem_limit_bytes=48 * 1024 * 1024
        ),
        cost_estimate=pl.CostEstimate(flops=4 << 30, bytes_accessed=300 << 20, transcendentals=0),
    )(data, pick)


def coadd_kernel(total_ref, coadd_ref, term_ref):
    side = total_ref.shape[1]
    for ty in range(TILES_Y):
        for tx in range(TILES_X):
            tile = ty * TILES_X + tx
            numer = total_ref[pl.ds(tile, side, stride=2 * TILES), :]
            denom = total_ref[pl.ds(TILES + tile, side, stride=2 * TILES), :]
            coadd = numer / jnp.maximum(denom, FLOOR)
            spot = (slice(ty * side, (ty + 1) * side), slice(tx * side, (tx + 1) * side))
            coadd_ref[spot] = coadd
            term_ref[spot] = numer * coadd


def per_device(images, coeffs, inverse_var, bad_lines, destinations, tile_slots):
    owners_count = lax.axis_size("patch")
    piece_count = images.shape[1]
    if owners_count != 8 or piece_count != 32 or lax.axis_size("band") != 4:
        return exchanged_raw(images, coeffs, inverse_var, bad_lines, destinations, tile_slots)
    tile_side = inverse_var.shape[-1]
    half_taps = (images.shape[-1] - tile_side) // 2
    bands = fixed_bands(tile_side, half_taps)
    labels = destinations[0, :, 0] * TILES + tile_slots[0]
    data = match_local(images[0], coeffs[0], inverse_var[0], bad_lines[0], bands)
    total = exchange_line(data, labels)
    shape = jax.ShapeDtypeStruct((TILES_Y * tile_side, TILES_X * tile_side), jnp.float32)
    coadd, terms = pl.pallas_call(
        coadd_kernel,
        out_shape=(shape, shape),
        compiler_params=pltpu.CompilerParams(vmem_limit_bytes=32 * 1024 * 1024),
    )(total.reshape(-1, tile_side))
    band = lax.axis_index("band")
    share = terms.shape[0] // 4

    def block(index):
        return lax.dynamic_slice_in_dim(terms, index * share, share, axis=0)

    arrived = [
        lax.ppermute(block(band ^ turn), "band", [(b, b ^ turn) for b in range(4)])
        for turn in (3, 1, 2)
    ]
    detection = block(band) + arrived[1] + arrived[2] + arrived[0]
    return (coadd[None, None], detection[None])


def solution(mesh):
    in_specs = (
        P("band", "patch", None, None),
        P("band", "patch", None, None, None),
        P("band", "patch", None, None),
        P("band", "patch", None),
        P("band", "patch", None),
        P("band", "patch"),
    )
    out_specs = (P("band", "patch", None, None), P("patch", "band", None))
    return jax.shard_map(
        per_device, mesh=mesh, in_specs=in_specs, out_specs=out_specs, check_vma=False
    )
```
